512 devices in a mesh: blk: 64 (over z, y_lo, x), layer: 8 (over y_hi, core).
Axes of the slice: x: 4, y: 8 (y_hi: 4, y_lo: 2; y = y_hi * 2 + y_lo), z: 8, core: 2. Of those that a mesh axis runs over, the one named last changes fastest.
Arguments:
- points: bfloat16 [65536, 128], P('blk'), may hold values from -12 to 12, as said below
- directions: bfloat16 [65536, 64], P('blk'), may hold values from -0.09375 to 0.09375
Outputs:
- product: float32 [65536, 64], P(('blk', 'layer'))
The draws below stay inside these ranges and needn't reach their ends.
Inputs may be any that keep to these rules, and one draw needn't show every extreme that they name: `points`: embeddings with row scales that differ from row to row.
All inputs are finite; a program needn't handle non-finite values.
Results may differ from the reference program's by a relative error of at most 0.0033.
Values may be sent and summed in bfloat16 or wider, within the bound.
A program may use at most 64 MiB of HBM per device.

```python
import jax
import jax.numpy as jnp
from jax import lax

DIMS = 128
RHS = 64
ROWS_DEV = 1024
TOKENS = 65536


def draw_points(key, part):
    key = jax.random.fold_in(key, 1)
    first, second, third, fourth = jax.random.split(key, 4)
    loading = 0.35 * jax.random.truncated_normal(second, -3.0, 3.0, (8, DIMS), jnp.float32)
    coords = jax.random.truncated_normal(first, -4.0, 4.0, (TOKENS, 8), jnp.float32)
    jitter = 1.7 * jax.random.truncated_normal(third, -4.0, 4.0, (TOKENS, DIMS), jnp.float32)
    base = jitter
    for column in range(8):
        base = base + coords[:, column:column + 1] * loading[column][None, :]
    scales = jnp.exp(jax.random.uniform(fourth, (TOKENS,), jnp.float32, jnp.log(0.4), jnp.log(1.2)))
    return jnp.clip(base * scales[:, None], -12.0, 12.0).astype(jnp.bfloat16)


def shard_levels(stream_key, extent, shards, least, top_value):
    factor_of, own = 1.0, jax.random.fold_in(stream_key, 6)
    for axis_at, shards_of in shards:
        draws = jnp.exp(jax.random.uniform(jax.random.fold_in(own, axis_at), (shards_of,), jnp.float32, least / len(shards), top_value / len(shards)))
        factor_of = factor_of * jnp.repeat(draws, extent[axis_at] // shards_of).reshape([-1 if axis == axis_at else 1 for axis in range(len(extent))])
    return factor_of


def bell_draw(key, dims, spread, limit, pieces=(), kind=jnp.bfloat16):
    values = spread * jax.random.normal(key, dims, jnp.float32)
    if pieces:
        values = values * shard_levels(key, dims, pieces, -0.22, 0.18)
    return jnp.clip(values, -limit, limit).astype(kind)


def setup_inputs(seed: int = 0) -> dict:
    streams_of = jax.random.split(jax.random.key(seed), 3)
    points = draw_points(jax.random.fold_in(streams_of[2], 71), 0)
    directions = bell_draw(streams_of[1], (TOKENS, RHS), (4.0 / TOKENS ** 0.5), 0.09375, ((0, 64),))
    return dict(points=points, directions=directions)


def reference(points, directions):
    gamma = 0.5 / points.shape[1]
    wide = points.astype(jnp.float32)
    norms = jnp.sum(wide * wide, axis=1)
    point_blocks = points.reshape(TOKENS // ROWS_DEV, ROWS_DEV, DIMS)
    norm_blocks = norms.reshape(TOKENS // ROWS_DEV, ROWS_DEV)

    def one_block(pair):
        block_points, block_norms = pair
        gram = jnp.dot(block_points, points.T, preferred_element_type=jnp.float32)
        dist = jnp.maximum(block_norms[:, None] + norms[None, :] - 2.0 * gram, 0.0)
        kernel = jnp.exp(-gamma * dist).astype(jnp.bfloat16)
        return jnp.dot(kernel, directions, preferred_element_type=jnp.float32)

    result = lax.map(one_block, (point_blocks, norm_blocks))
    return result.reshape(TOKENS, RHS)
```

```python
import functools

import numpy as np

import jax
import jax.numpy as jnp
from jax import lax
from jax.experimental import pallas as pl
from jax.experimental.pallas import tpu as pltpu
from jax.sharding import PartitionSpec as P

MESH = pl.DeviceIdType.MESH
BF = jnp.bfloat16
F32 = jnp.float32

NX, NP, NZ, NK = 4, 2, 8, 4
ROWS, FEATS, RHS = 1024, 128, 64
HALF = ROWS // 2
LANES = 128
GROUPS = 8
PACK = HALF // GROUPS
WIDTH = LANES // GROUPS
TILES = HALF // LANES
MSG = HALF + TILES * RHS + PACK
DEPTH = 2 * FEATS
LOG2E = float(np.log2(np.e))


def pieces(value):
    first = value.astype(BF).astype(F32)
    rest = value - first
    second = rest.astype(BF).astype(F32)
    third = (rest - second).astype(BF).astype(F32)
    return first, second, third


def choose(index, values, others):
    result = others
    for at, value in values:
        result = jnp.where(index == at, value, result)
    return result


def kernel(scale, pts, dirs, out, rbuf, msg, cbuf, maug, acc, obuf, stage, fin, ybuf, send, recv):
    blk, layer = lax.axis_index("blk"), lax.axis_index("layer")
    x, p, z = blk % NX, (blk // NX) % NP, blk // (NX * NP)
    k, c = layer // 2, layer % 2
    near = jnp.where(k == 0, 0, jnp.where(k == 1, 1, jnp.where(k == 2, 7, 2)))

    def at(xx=x, pp=p, zz=z, kk=k, cc=c):
        return ((zz * NP + pp) * NX + xx, kk * 2 + cc)

    def along_x(by):
        return at(xx=lax.rem(x + by, NX))

    def along_z(by):
        return at(zz=lax.rem(z + by + 2 * NZ, NZ))

    def along_k(by):
        return at(kk=lax.rem(k + by, NK))

    mate = at(cc=1 - c)
    pair_near = at(pp=1 - p)
    pair_far = at(pp=1 - p, kk=lax.rem(k + 2 * p - 1 + NK, NK))

    barrier = pltpu.get_barrier_semaphore()

    def greet(device):
        pl.semaphore_signal(barrier, inc=1, device_id=device, device_id_type=MESH)

    for by in range(1, NX):
        greet(along_x(by))
    for by in range(1, NK):
        greet(along_k(by))
    greet(mate)
    greet(pair_near)
    greet(pair_far)
    greet(along_z(near + 4))

    @pl.when(k != 0)
    def _():
        greet(along_z(near))

    for h in range(NK):
        rows = pts[pl.ds(pl.multiple_of((2 * h + c) * LANES, LANES), LANES), :]
        turned = rows.astype(F32).T
        rbuf[0, 0:FEATS, h * LANES:(h + 1) * LANES] = turned.astype(BF)
        norm = -0.5 * jnp.sum(turned * turned, axis=0, keepdims=True)
        first, second, third = pieces(norm)
        row = lax.broadcasted_iota(jnp.int32, (WIDTH, LANES), 0)
        extra = choose(
            row, [(0, first), (1, second), (2, third)], jnp.where(row < 6, 1.0, 0.0)
        )
        rbuf[0, FEATS:FEATS + WIDTH, h * LANES:(h + 1) * LANES] = extra.astype(BF)

    lane = lax.broadcasted_iota(jnp.int32, (PACK, LANES), 1)
    packed = jnp.zeros((PACK, LANES), F32)
    for g in range(GROUPS):
        rows = pts[pl.ds(pl.multiple_of(c * HALF + g * PACK, PACK), PACK), :]
        msg[g * PACK:(g + 1) * PACK, :] = rows
        wide = rows.astype(F32)
        norm = -0.5 * jnp.sum(wide * wide, axis=1, keepdims=True)
        packed = jnp.where(lane // WIDTH == g, norm, packed)
    for t in range(TILES):
        cols = pl.ds(pl.multiple_of(c * HALF + t * LANES, LANES), LANES)
        msg[HALF + t * RHS:HALF + (t + 1) * RHS, :] = dirs[:, cols]
    first, second, third = pieces(packed)
    place = lane % WIDTH
    extra = choose(
        place, [(3, first), (4, second), (5, third)], jnp.where(place < 3, 1.0, 0.0)
    )
    msg[HALF + TILES * RHS:MSG, :] = extra.astype(BF)

    pl.semaphore_wait(barrier, jnp.where(k == 0, 10, 11))

    def copy(n, src, dst, device):
        return pltpu.make_async_remote_copy(
            src_ref=src,
            dst_ref=dst,
            send_sem=send.at[n],
            recv_sem=recv.at[n],
            device_id=device,
            device_id_type=MESH,
        )

    z_near = copy(0, msg, cbuf.at[0, 0], along_z(-near))
    z_far = copy(1, msg, cbuf.at[2, 0], along_z(-near - 4))
    own = pltpu.make_async_copy(msg, cbuf.at[0, 0], recv.at[0])
    y_near = copy(2, cbuf.at[0, 0], cbuf.at[1, 0], pair_near)
    y_far = copy(3, cbuf.at[2, 0], cbuf.at[3, 0], pair_far)
    shared = [copy(4 + s, cbuf.at[s, 0], cbuf.at[s, 1], mate) for s in range(4)]
    r_used = pl.ds(0, FEATS + WIDTH)
    rows_x = [
        copy(8 + by, rbuf.at[0, r_used], rbuf.at[by, r_used], along_x(by)) for by in range(1, NX)
    ]
    back_x = [
        copy(11 + by, stage.at[by - 1], obuf.at[by - 1], along_x(NX - by)) for by in range(1, NX)
    ]
    back_k = [
        copy(14 + by, fin.at[lax.rem(k + by, NK)], ybuf.at[by - 1], along_k(by))
        for by in range(1, NK)
    ]

    @pl.when(k != 0)
    def _():
        z_near.start()

    @pl.when(k == 0)
    def _():
        own.start()

    for by in (1, 3, 2):
        rows_x[by - 1].start()
    z_far.start()

    masks = [jnp.where(lane // WIDTH == g, 1.0, 0.0).astype(BF) for g in range(GROUPS)]

    def spread_norms(s, half):
        tile = cbuf[s, half, HALF + TILES * RHS:MSG, :]
        for g in range(GROUPS):
            maug[s, half * HALF + g * PACK:half * HALF + (g + 1) * PACK, :] = tile * masks[g]

    def spread_rows(by):
        tile = rbuf[by, FEATS:FEATS + WIDTH, :]
        for g in range(1, GROUPS):
            rbuf[by, FEATS + g * WIDTH:FEATS + (g + 1) * WIDTH, :] = tile

    def product(sources, by):
        left = jnp.concatenate(
            [
                jnp.concatenate([cbuf[s, half, 0:HALF, :] for s in sources for half in range(2)], axis=0),
                jnp.concatenate([maug[s] for s in sources], axis=0),
            ],
            axis=1,
        )
        weights = jnp.concatenate(
            [
                cbuf[s, half, HALF + t * RHS:HALF + (t + 1) * RHS, :]
                for s in sources
                for half in range(2)
                for t in range(TILES)
            ],
            axis=1,
        )
        power = jnp.dot(left, rbuf[by], preferred_element_type=F32)
        value = jnp.minimum(jnp.exp2(power * scale).astype(BF), jnp.ones((), BF))
        return jnp.dot(weights, value, preferred_element_type=F32)

    spread_rows(0)
    z_near.wait_recv()
    y_near.start()
    shared[0].start()
    spread_norms(0, 0)
    for by in (1, 3, 2):
        rows_x[by - 1].wait_recv()
        spread_rows(by)
    shared[0].wait_recv()
    spread_norms(0, 1)
    for by in range(NX):
        acc[by] = product((0,), by)

    y_near.wait_recv()
    shared[1].start()
    spread_norms(1, 0)
    z_far.wait_recv()
    y_far.start()
    shared[2].start()
    spread_norms(2, 0)
    shared[1].wait_recv()
    spread_norms(1, 1)
    for by in range(NX):
        acc[by] += product((1,), by)

    y_far.wait_recv()
    shared[3].start()
    spread_norms(3, 0)
    shared[2].wait_recv()
    spread_norms(2, 1)
    shared[3].wait_recv()
    spread_norms(3, 1)
    for by in (2, 1, 3):
        stage[by - 1] = (acc[by] + product((2, 3), by)).astype(BF)
        back_x[by - 1].start()
    total = acc[0] + product((2, 3), 0)
    for by in (2, 1, 3):
        back_x[by - 1].wait_recv()
        total += obuf[by - 1].astype(F32)
    for h in range(NK):
        fin[h] = total[:, h * LANES:(h + 1) * LANES]
    for by in range(1, NK):
        back_k[by - 1].start()
    result = fin[k]
    for by in range(1, NK):
        back_k[by - 1].wait_recv()
        result += ybuf[by - 1]
    out[...] = result

    @pl.when(k != 0)
    def _():
        z_near.wait_send()

    for one in (z_far, y_near, y_far, *shared, *rows_x, *back_x, *back_k):
        one.wait_send()


def local(points, directions):
    gamma = 0.5 / points.shape[1]
    turned = pl.pallas_call(
        functools.partial(kernel, 2.0 * gamma * LOG2E),
        out_shape=jax.ShapeDtypeStruct((RHS, LANES), F32),
        in_specs=[pl.BlockSpec(memory_space=pltpu.VMEM)] * 2,
        out_specs=pl.BlockSpec(memory_space=pltpu.VMEM),
        scratch_shapes=[
            pltpu.VMEM((NX, DEPTH, HALF), BF),
            pltpu.VMEM((MSG, LANES), BF),
            pltpu.VMEM((4, 2, MSG, LANES), BF),
            pltpu.VMEM((4, ROWS, LANES), BF),
            pltpu.VMEM((NX, RHS, HALF), F32),
            pltpu.VMEM((NX - 1, RHS, HALF), BF),
            pltpu.VMEM((NX - 1, RHS, HALF), BF),
            pltpu.VMEM((NK, RHS, LANES), F32),
            pltpu.VMEM((NK - 1, RHS, LANES), F32),
            pltpu.SemaphoreType.DMA((18,)),
            pltpu.SemaphoreType.DMA((18,)),
        ],
        compiler_params=pltpu.CompilerParams(
            collective_id=0, has_side_effects=True, vmem_limit_bytes=48 * 2**20
        ),
        name="gauss",
    )(points, directions.T)
    return turned.T


def solution(mesh):
    in_specs = (P("blk", None), P("blk", None))
    out_specs = P(("blk", "layer"), None)
    return jax.shard_map(local, mesh=mesh, in_specs=in_specs, out_specs=out_specs, check_vma=False)
```

```python
import functools

import numpy as np

import jax
import jax.numpy as jnp
from jax import lax
from jax.experimental import pallas as pl
from jax.experimental.pallas import tpu as pltpu
from jax.sharding import PartitionSpec as P

MESH = pl.DeviceIdType.MESH
BF = jnp.bfloat16
F32 = jnp.float32

NX, NP, NZ, NK = 4, 2, 8, 4
ROWS, FEATS, RHS = 1024, 128, 64
HALF = ROWS // 2
LANES = 128
PARTS = 2
PART = HALF // PARTS
GROUPS = 8
PACK = PART // GROUPS
WIDTH = LANES // GROUPS
TILES = PART // LANES
NORMS = PART + TILES * RHS
MSG = NORMS + PACK
DEPTH = 2 * FEATS
LOG2E = float(np.log2(np.e))


def pieces(value):
    first = value.astype(BF).astype(F32)
    rest = value - first
    second = rest.astype(BF).astype(F32)
    third = (rest - second).astype(BF).astype(F32)
    return first, second, third


def choose(index, values, others):
    result = others
    for at, value in values:
        result = jnp.where(index == at, value, result)
    return result


def kernel(scale, pts_hbm, dirs_hbm, out, pts, dirs, msg, rbuf, cbuf, maug, acc, stage, obuf, fin, ybuf, load, send, recv):
    blk, layer = lax.axis_index("blk"), lax.axis_index("layer")
    x, p, z = blk % NX, (blk // NX) % NP, blk // (NX * NP)
    k, c = layer // 2, layer % 2
    turn = jnp.where((k == 1) | (k == 2), c, 0)
    near = choose(k, [(0, 0), (1, 1 + 6 * turn), (2, 7 - 6 * turn)], 2)

    def at(xx=x, pp=p, zz=z, kk=k, cc=c):
        return ((zz * NP + pp) * NX + xx, kk * 2 + cc)

    def along_x(by):
        return at(xx=(x + by) % NX)

    def along_z(by):
        return at(zz=(z + by + 2 * NZ) % NZ)

    def along_k(by):
        return at(kk=(k + by) % NK)

    mate = at(cc=1 - c)
    pair_k = (k + c * (2 * p - 1) + NK) % NK

    def across(by):
        return at(xx=(x + by) % NX, pp=1 - p, kk=pair_k)

    barrier = pltpu.get_barrier_semaphore()

    def greet(device):
        pl.semaphore_signal(barrier, inc=1, device_id=device, device_id_type=MESH)

    greet(along_z(near + 4))

    @pl.when(k != 0)
    def _():
        greet(along_z(near))

    for by in range(1, NK):
        greet(along_k(by))
    for by in range(1, NX):
        greet(along_x(by))
    for by in range(NX):
        greet(across(by))
    greet(mate)

    load_pts = pltpu.make_async_copy(pts_hbm, pts, load.at[0])
    load_dirs = pltpu.make_async_copy(dirs_hbm, dirs, load.at[1])
    load_pts.start()
    load_dirs.start()
    load_pts.wait()

    row = lax.broadcasted_iota(jnp.int32, (WIDTH, LANES), 0)
    for h in range(NK):
        rows = pts[pl.ds(pl.multiple_of((2 * h + c) * LANES, LANES), LANES), :]
        turned = rows.astype(F32).T
        rbuf[0, 0:FEATS, h * LANES:(h + 1) * LANES] = turned.astype(BF)
        norm = -0.5 * jnp.sum(turned * turned, axis=0, keepdims=True)
        first, second, third = pieces(norm)
        extra = choose(
            row, [(0, first), (1, second), (2, third)], jnp.where(row < 6, 1.0, 0.0)
        ).astype(BF)
        for g in range(GROUPS):
            rbuf[0, FEATS + g * WIDTH:FEATS + (g + 1) * WIDTH, h * LANES:(h + 1) * LANES] = extra

    load_dirs.wait()
    lane = lax.broadcasted_iota(jnp.int32, (PACK, LANES), 1)
    place = lane % WIDTH
    for q in range(PARTS):
        packed = jnp.zeros((PACK, LANES), F32)
        for g in range(GROUPS):
            start = pl.multiple_of(c * HALF + q * PART + g * PACK, PACK)
            rows = pts[pl.ds(start, PACK), :]
            msg[q, g * PACK:(g + 1) * PACK, :] = rows
            wide = rows.astype(F32)
            norm = -0.5 * jnp.sum(wide * wide, axis=1, keepdims=True)
            packed = jnp.where(lane // WIDTH == g, norm, packed)
        for t in range(TILES):
            cols = pl.ds(pl.multiple_of(c * HALF + q * PART + t * LANES, LANES), LANES)
            msg[q, PART + t * RHS:PART + (t + 1) * RHS, :] = dirs[:, cols]
        first, second, third = pieces(packed)
        extra = choose(
            place, [(3, first), (4, second), (5, third)], jnp.where(place < 3, 1.0, 0.0)
        )
        msg[q, NORMS:MSG, :] = extra.astype(BF)

    pl.semaphore_wait(barrier, jnp.where(k == 0, 12, 13))

    def copy(n, src, dst, device):
        return pltpu.make_async_remote_copy(
            src_ref=src,
            dst_ref=dst,
            send_sem=send.at[n],
            recv_sem=recv.at[n],
            device_id=device,
            device_id_type=MESH,
        )

    parts = range(PARTS)
    z_near = [copy(q, msg.at[q], cbuf.at[0, 0, q], along_z(-near)) for q in parts]
    z_own = [pltpu.make_async_copy(msg.at[q], cbuf.at[0, 0, q], recv.at[q]) for q in parts]
    z_far = [copy(4 + q, msg.at[q], cbuf.at[1, 0, q], along_z(-near - 4)) for q in parts]
    shared = [
        [copy(8 + 4 * n + q, cbuf.at[n, 0, q], cbuf.at[n, 1, q], mate) for q in parts]
        for n in range(2)
    ]
    r_used = pl.ds(0, FEATS + WIDTH)
    rows_x = [
        copy(15 + by, rbuf.at[0, r_used], rbuf.at[by, r_used], along_x(by)) for by in range(1, NX)
    ]
    rows_y = [
        copy(19 + by, rbuf.at[by, r_used], rbuf.at[NX + by, r_used], across(0)) for by in range(NX)
    ]
    back_x = {
        by: copy(23 + by, stage.at[by], obuf.at[by], along_x(NX - by) if by < NX else across(2 * NX - by))
        for by in range(1, 2 * NX)
    }
    back_k = [
        copy(30 + by, fin.at[(k + by) % NK], ybuf.at[by - 1], along_k(by)) for by in range(1, NK)
    ]

    @pl.when(k != 0)
    def _():
        for one in z_near:
            one.start()

    @pl.when(k == 0)
    def _():
        for one in z_own:
            one.start()

    for by in (1, 3, 2):
        rows_x[by - 1].start()
    rows_y[0].start()
    for one in z_far:
        one.start()

    masks = [jnp.where(lane // WIDTH == g, 1.0, 0.0).astype(BF) for g in range(GROUPS)]

    def spread_norms(n, half):
        for q in parts:
            tile = cbuf[n, half, q, NORMS:MSG, :]
            for g in range(GROUPS):
                first = half * HALF + q * PART + g * PACK
                maug[n, first:first + PACK, :] = tile * masks[g]

    def pass_on(n, arrives, leave):
        for q in parts:
            arrives[q].wait_recv()
            for one in leave:
                one[q].start()
        spread_norms(n, 0)

    def from_mate(n):
        for one in shared[n]:
            one.wait_recv()
        spread_norms(n, 1)

    def spread_rows(by):
        tile = rbuf[by, FEATS:FEATS + WIDTH, :]
        for g in range(1, GROUPS):
            rbuf[by, FEATS + g * WIDTH:FEATS + (g + 1) * WIDTH, :] = tile

    def product(sources, by):
        pieces_of = [(n, half, q) for n in sources for half in range(2) for q in parts]
        lhs = jnp.concatenate(
            [
                jnp.concatenate([cbuf[n, half, q, 0:PART, :] for n, half, q in pieces_of], axis=0),
                jnp.concatenate([maug[n] for n in sources], axis=0),
            ],
            axis=1,
        )
        weights = jnp.concatenate(
            [
                cbuf[n, half, q, PART + t * RHS:PART + (t + 1) * RHS, :]
                for n, half, q in pieces_of
                for t in range(TILES)
            ],
            axis=1,
        )
        power = jnp.dot(lhs, rbuf[by], preferred_element_type=F32)
        value = jnp.minimum(jnp.exp2(power * scale).astype(BF), jnp.ones((), BF))
        return jnp.dot(weights, value, preferred_element_type=F32)

    for by in (1, 3, 2):
        rows_x[by - 1].wait_recv()
        rows_y[by].start()
        spread_rows(by)
    pass_on(0, z_near, (shared[0],))
    from_mate(0)
    for by in range(NX):
        acc[by] = product((0,), by)

    for by in range(NX):
        rows_y[by].wait_recv()
        spread_rows(NX + by)
    pass_on(1, z_far, (shared[1],))
    for by in range(NX, 2 * NX):
        acc[by] = product((0,), by)

    from_mate(1)
    for group in ((6, 2), (5, 1), (7, 3), (4,)):
        for by in group:
            stage[by] = (acc[by] + product((1,), by)).astype(BF)
        for by in group:
            back_x[by].start()
    total = acc[0] + product((1,), 0)
    for by in (6, 2, 5, 1, 7, 3, 4):
        back_x[by].wait_recv()
        total += obuf[by].astype(F32)
    for h in range(NK):
        fin[h] = total[:, h * LANES:(h + 1) * LANES].astype(BF)
        acc[0, :, h * LANES:(h + 1) * LANES] = total[:, h * LANES:(h + 1) * LANES]
    for by in (2, 1, 3):
        back_k[by - 1].start()
    result = acc[0, :, pl.ds(pl.multiple_of(k * LANES, LANES), LANES)]
    for by in (1, 3, 2):
        back_k[by - 1].wait_recv()
        result += ybuf[by - 1].astype(F32)
    out[...] = result

    @pl.when(k != 0)
    def _():
        for one in z_near:
            one.wait_send()

    groups = (z_far, *shared, rows_x, rows_y, back_x.values(), back_k)
    for group in groups:
        for one in group:
            one.wait_send()


def local(points, directions):
    gamma = 0.5 / points.shape[1]
    turned = pl.pallas_call(
        functools.partial(kernel, 2.0 * gamma * LOG2E),
        out_shape=jax.ShapeDtypeStruct((RHS, LANES), F32),
        in_specs=[pl.BlockSpec(memory_space=pl.ANY)] * 2,
        out_specs=pl.BlockSpec(memory_space=pltpu.VMEM),
        scratch_shapes=[
            pltpu.VMEM((ROWS, FEATS), BF),
            pltpu.VMEM((RHS, ROWS), BF),
            pltpu.VMEM((PARTS, MSG, LANES), BF),
            pltpu.VMEM((2 * NX, DEPTH, HALF), BF),
            pltpu.VMEM((2, 2, PARTS, MSG, LANES), BF),
            pltpu.VMEM((2, ROWS, LANES), BF),
            pltpu.VMEM((2 * NX, RHS, HALF), F32),
            pltpu.VMEM((2 * NX, RHS, HALF), BF),
            pltpu.VMEM((2 * NX, RHS, HALF), BF),
            pltpu.VMEM((NK, RHS, LANES), BF),
            pltpu.VMEM((NK - 1, RHS, LANES), BF),
            pltpu.SemaphoreType.DMA((2,)),
            pltpu.SemaphoreType.DMA((34,)),
            pltpu.SemaphoreType.DMA((34,)),
        ],
        compiler_params=pltpu.CompilerParams(
            collective_id=0, has_side_effects=True, vmem_limit_bytes=60 * 2**20
        ),
        name="gauss",
    )(points, directions.T)
    return turned.T


def solution(mesh):
    in_specs = (P("blk", None), P("blk", None))
    out_specs = P(("blk", "layer"), None)
    return jax.shard_map(local, mesh=mesh, in_specs=in_specs, out_specs=out_specs, check_vma=False)
```

```python
import functools

import numpy as np

import jax
import jax.numpy as jnp
from jax import lax
from jax.experimental import pallas as pl
from jax.experimental.pallas import tpu as pltpu
from jax.sharding import PartitionSpec as P

MESH = pl.DeviceIdType.MESH
BF = jnp.bfloat16
F32 = jnp.float32

NX, NP, NZ, NK = 4, 2, 8, 4
ROWS, FEATS, RHS = 1024, 128, 64
HALF = ROWS // 2
LANES = 128
QUARTER = ROWS // NK
PART = QUARTER // 2
GROUPS = 8
PACK = PART // GROUPS
WIDTH = LANES // GROUPS
TILES = PART // LANES
NORMS = PART + TILES * RHS
MSG = NORMS + PACK
DEPTH = 2 * FEATS
LOG2E = float(np.log2(np.e))


def pieces(value):
    first = value.astype(BF).astype(F32)
    rest = value - first
    second = rest.astype(BF).astype(F32)
    third = (rest - second).astype(BF).astype(F32)
    return first, second, third


def choose(index, values, others):
    result = others
    for at, value in values:
        result = jnp.where(index == at, value, result)
    return result


def kernel(scale, pts_hbm, dirs_hbm, out, pts, dirs, rbuf, cbuf, maug, acc, stage, obuf, fin, ybuf, load, send, recv):
    blk, layer = lax.axis_index("blk"), lax.axis_index("layer")
    x, p, z = blk % NX, (blk // NX) % NP, blk // (NX * NP)
    k, c = layer // 2, layer % 2

    def at(xx=x, pp=p, zz=z, kk=k, cc=c):
        return ((zz * NP + pp) * NX + xx, kk * 2 + cc)

    def along_x(by):
        return at(xx=(x + by) % NX)

    def along_z(by):
        return at(zz=(z + by + 2 * NZ) % NZ)

    def along_k(by):
        return at(kk=(k + by) % NK)

    mate = at(cc=1 - c)
    pair_k = (k + c * (2 * p - 1) + NK) % NK

    def across(by):
        return at(xx=(x + by) % NX, pp=1 - p, kk=pair_k)

    barrier = pltpu.get_barrier_semaphore()

    def greet(device):
        pl.semaphore_signal(barrier, inc=1, device_id=device, device_id_type=MESH)

    for by in (2, -2, 1, -1):
        greet(along_z(by))
    for by in range(1, NK):
        greet(along_k(by))
    for by in range(1, NX):
        greet(along_x(by))
    for by in range(NX):
        greet(across(by))
    greet(mate)

    load_pts = pltpu.make_async_copy(pts_hbm, pts, load.at[0])
    load_dirs = pltpu.make_async_copy(dirs_hbm, dirs, load.at[1])
    load_pts.start()
    load_dirs.start()
    load_pts.wait()

    row = lax.broadcasted_iota(jnp.int32, (WIDTH, LANES), 0)
    for h in range(NK):
        rows = pts[pl.ds(pl.multiple_of((2 * h + c) * LANES, LANES), LANES), :]
        turned = rows.astype(F32).T
        rbuf[0, 0:FEATS, h * LANES:(h + 1) * LANES] = turned.astype(BF)
        norm = -0.5 * jnp.sum(turned * turned, axis=0, keepdims=True)
        first, second, third = pieces(norm)
        extra = choose(
            row, [(0, first), (1, second), (2, third)], jnp.where(row < 6, 1.0, 0.0)
        ).astype(BF)
        for g in range(GROUPS):
            rbuf[0, FEATS + g * WIDTH:FEATS + (g + 1) * WIDTH, h * LANES:(h + 1) * LANES] = extra

    load_dirs.wait()
    lane = lax.broadcasted_iota(jnp.int32, (PACK, LANES), 1)
    place = lane % WIDTH
    for half in range(2):
        base = k * QUARTER + lax.rem(c + half, 2) * PART
        packed = jnp.zeros((PACK, LANES), F32)
        for g in range(GROUPS):
            rows = pts[pl.ds(pl.multiple_of(base + g * PACK, PACK), PACK), :]
            cbuf[0, half, g * PACK:(g + 1) * PACK, :] = rows
            wide = rows.astype(F32)
            norm = -0.5 * jnp.sum(wide * wide, axis=1, keepdims=True)
            packed = jnp.where(lane // WIDTH == g, norm, packed)
        cbuf[0, half, PART:NORMS, :] = dirs[:, pl.ds(pl.multiple_of(base, LANES), LANES)]
        first, second, third = pieces(packed)
        extra = choose(
            place, [(3, first), (4, second), (5, third)], jnp.where(place < 3, 1.0, 0.0)
        )
        cbuf[0, half, NORMS:MSG, :] = extra.astype(BF)

    pl.semaphore_wait(barrier, 15)

    def copy(n, src, dst, device):
        return pltpu.make_async_remote_copy(
            src_ref=src,
            dst_ref=dst,
            send_sem=send.at[n],
            recv_sem=recv.at[n],
            device_id=device,
            device_id_type=MESH,
        )

    along = {by: copy(by, cbuf.at[0, 0], cbuf.at[by, 0], along_z(-by)) for by in (1, 2, 6, 7)}
    along[3] = copy(3, cbuf.at[2, 0], cbuf.at[3, 0], along_z(-1))
    along[5] = copy(5, cbuf.at[6, 0], cbuf.at[5, 0], along_z(1))
    along[4] = copy(4, cbuf.at[6 - 4 * c, 0], cbuf.at[4, 0], along_z(2 - 4 * c))
    shared = {by: copy(7 + by, cbuf.at[by, 0], cbuf.at[by, 1], mate) for by in range(1, NZ)}
    r_used = pl.ds(0, FEATS + WIDTH)
    rows_x = [
        copy(15 + by, rbuf.at[0, r_used], rbuf.at[by, r_used], along_x(by)) for by in range(1, NX)
    ]
    rows_y = [
        copy(19 + by, rbuf.at[by, r_used], rbuf.at[NX + by, r_used], across(0)) for by in range(NX)
    ]
    back_x = {
        by: copy(23 + by, stage.at[by], obuf.at[by], along_x(NX - by) if by < NX else across(2 * NX - by))
        for by in range(1, 2 * NX)
    }
    back_k = [
        copy(30 + by, fin.at[(k + by) % NK], ybuf.at[by - 1], along_k(by)) for by in range(1, NK)
    ]

    for by in (2, 6, 1, 7):
        along[by].start()
    for by in (1, 3):
        rows_x[by - 1].start()
    rows_y[0].start()
    rows_x[1].start()

    masks = [jnp.where(lane // WIDTH == g, 1.0, 0.0).astype(BF) for g in range(GROUPS)]

    def spread_norms(by, half):
        tile = cbuf[by, half, NORMS:MSG, :]
        for g in range(GROUPS):
            first = half * PART + g * PACK
            maug[by, first:first + PACK, :] = tile * masks[g]

    def pass_on(offsets, onward):
        for by in offsets:
            along[by].wait_recv()
        for by in onward:
            along[by].start()
        for by in offsets:
            shared[by].start()
        for by in offsets:
            spread_norms(by, 0)

    def from_mate(*offsets):
        for by in offsets:
            shared[by].wait_recv()
            spread_norms(by, 1)

    def spread_rows(by):
        tile = rbuf[by, FEATS:FEATS + WIDTH, :]
        for g in range(1, GROUPS):
            rbuf[by, FEATS + g * WIDTH:FEATS + (g + 1) * WIDTH, :] = tile

    def product(sources, by):
        halves = [(n, half) for n in sources for half in range(2)]
        lhs = jnp.concatenate(
            [
                jnp.concatenate([cbuf[n, half, 0:PART, :] for n, half in halves], axis=0),
                jnp.concatenate([maug[n] for n in sources], axis=0),
            ],
            axis=1,
        )
        weights = jnp.concatenate([cbuf[n, half, PART:NORMS, :] for n, half in halves], axis=1)
        power = jnp.dot(lhs, rbuf[by], preferred_element_type=F32)
        value = jnp.minimum(jnp.exp2(power * scale).astype(BF), jnp.ones((), BF))
        return jnp.dot(weights, value, preferred_element_type=F32)

    spread_norms(0, 0)
    spread_norms(0, 1)
    pass_on((1, 7), ())
    for by in (1, 3):
        rows_x[by - 1].wait_recv()
        rows_y[by].start()
        spread_rows(by)
    pass_on((2, 6), (3, 5, 4))
    rows_y[0].wait_recv()
    spread_rows(4)
    from_mate(1, 7, 2, 6)
    close = (0, 1, 7, 2, 6)
    for by in (1, 3, 4):
        acc[by] = product(close, by)

    rows_x[1].wait_recv()
    rows_y[2].start()
    spread_rows(2)
    acc[2] = product(close, 2)
    for by in (1, 3):
        rows_y[by].wait_recv()
        spread_rows(NX + by)
    for by in (5, 7):
        acc[by] = product(close, by)

    pass_on((3, 5, 4), ())
    from_mate(3, 5, 4)
    rest = (3, 5, 4)

    def give(*group):
        for by in group:
            value = product(close + rest, by) if by == 6 else acc[by] + product(rest, by)
            stage[by] = value.astype(BF)
        for by in group:
            back_x[by].start()

    give(5, 2)
    rows_y[2].wait_recv()
    spread_rows(6)
    give(6)
    give(1, 7)
    give(3, 4)
    total = product(close + rest, 0)
    for by in (5, 2, 6, 1, 7, 3, 4):
        back_x[by].wait_recv()
        total += obuf[by].astype(F32)
    for h in range(NK):
        fin[h] = total[:, h * LANES:(h + 1) * LANES].astype(BF)
        acc[0, :, h * LANES:(h + 1) * LANES] = total[:, h * LANES:(h + 1) * LANES]
    for by in (2, 1, 3):
        back_k[by - 1].start()
    result = acc[0, :, pl.ds(pl.multiple_of(k * LANES, LANES), LANES)]
    for by in (1, 3, 2):
        back_k[by - 1].wait_recv()
        result += ybuf[by - 1].astype(F32)
    out[...] = result

    groups = (along.values(), shared.values(), rows_x, rows_y, back_x.values(), back_k)
    for group in groups:
        for one in group:
            one.wait_send()


def local(points, directions):
    gamma = 0.5 / points.shape[1]
    turned = pl.pallas_call(
        functools.partial(kernel, 2.0 * gamma * LOG2E),
        out_shape=jax.ShapeDtypeStruct((RHS, LANES), F32),
        in_specs=[pl.BlockSpec(memory_space=pl.ANY)] * 2,
        out_specs=pl.BlockSpec(memory_space=pltpu.VMEM),
        scratch_shapes=[
            pltpu.VMEM((ROWS, FEATS), BF),
            pltpu.VMEM((RHS, ROWS), BF),
            pltpu.VMEM((2 * NX, DEPTH, HALF), BF),
            pltpu.VMEM((NZ, 2, MSG, LANES), BF),
            pltpu.VMEM((NZ, QUARTER, LANES), BF),
            pltpu.VMEM((2 * NX, RHS, HALF), F32),
            pltpu.VMEM((2 * NX, RHS, HALF), BF),
            pltpu.VMEM((2 * NX, RHS, HALF), BF),
            pltpu.VMEM((NK, RHS, LANES), BF),
            pltpu.VMEM((NK - 1, RHS, LANES), BF),
            pltpu.SemaphoreType.DMA((2,)),
            pltpu.SemaphoreType.DMA((34,)),
            pltpu.SemaphoreType.DMA((34,)),
        ],
        compiler_params=pltpu.CompilerParams(
            collective_id=0, has_side_effects=True, vmem_limit_bytes=60 * 2**20
        ),
        name="gauss",
    )(points, directions.T)
    return turned.T


def solution(mesh):
    in_specs = (P("blk", None), P("blk", None))
    out_specs = P(("blk", "layer"), None)
    return jax.shard_map(local, mesh=mesh, in_specs=in_specs, out_specs=out_specs, check_vma=False)
```

```python
import functools

import numpy as np

import jax
import jax.numpy as jnp
from jax import lax
from jax.experimental import pallas as pl
from jax.experimental.pallas import tpu as pltpu
from jax.sharding import PartitionSpec as P

MESH = pl.DeviceIdType.MESH
BF = jnp.bfloat16
F32 = jnp.float32

NX, NP, NZ, NK = 4, 2, 8, 4
ROWS, FEATS, RHS = 1024, 128, 64
HALF = ROWS // 2
LANES = 128
QUARTER = ROWS // NK
PART = QUARTER // 2
GROUPS = 8
PACK = PART // GROUPS
WIDTH = LANES // GROUPS
TILES = PART // LANES
NORMS = PART + TILES * RHS
MSG = NORMS + PACK
DEPTH = 2 * FEATS
LOG2E = float(np.log2(np.e))


def pieces(value):
    first = value.astype(BF).astype(F32)
    rest = value - first
    second = rest.astype(BF).astype(F32)
    third = (rest - second).astype(BF).astype(F32)
    return first, second, third


def choose(index, values, others):
    result = others
    for at, value in values:
        result = jnp.where(index == at, value, result)
    return result


def kernel(scale, pts_hbm, dirs_hbm, out, pts, dirs, rbuf, cbuf, maug, acc, stage, obuf, fin, ybuf, load, send, recv):
    blk, layer = lax.axis_index("blk"), lax.axis_index("layer")
    x, p, z = blk % NX, (blk // NX) % NP, blk // (NX * NP)
    k, c = layer // 2, layer % 2

    def at(xx=x, pp=p, zz=z, kk=k, cc=c):
        return ((zz * NP + pp) * NX + xx, kk * 2 + cc)

    def along_x(by):
        return at(xx=(x + by) % NX)

    def along_z(by):
        return at(zz=(z + by + 2 * NZ) % NZ)

    def along_k(by):
        return at(kk=(k + by) % NK)

    mate = at(cc=1 - c)
    pair_k = (k + c * (2 * p - 1) + NK) % NK

    def across(by):
        return at(xx=(x + by) % NX, pp=1 - p, kk=pair_k)

    load_pts = pltpu.make_async_copy(pts_hbm, pts, load.at[0])
    load_dirs = pltpu.make_async_copy(dirs_hbm, dirs, load.at[1])
    load_pts.start()
    load_dirs.start()

    barrier = pltpu.get_barrier_semaphore()

    def greet(device):
        pl.semaphore_signal(barrier, inc=1, device_id=device, device_id_type=MESH)

    for by in (2, -2, 1, -1):
        greet(along_z(by))
    for by in range(1, NK):
        greet(along_k(by))
    for by in range(1, NX):
        greet(along_x(by))
    for by in range(NX):
        greet(across(by))
    greet(mate)

    load_pts.wait()

    row = lax.broadcasted_iota(jnp.int32, (WIDTH, LANES), 0)
    for h in range(NK):
        rows = pts[pl.ds(pl.multiple_of((2 * h + c) * LANES, LANES), LANES), :]
        turned = rows.astype(F32).T
        rbuf[0, 0:FEATS, h * LANES:(h + 1) * LANES] = turned.astype(BF)
        norm = -0.5 * jnp.sum(turned * turned, axis=0, keepdims=True)
        first, second, third = pieces(norm)
        extra = choose(
            row, [(0, first), (1, second), (2, third)], jnp.where(row < 6, 1.0, 0.0)
        ).astype(BF)
        for g in range(GROUPS):
            rbuf[0, FEATS + g * WIDTH:FEATS + (g + 1) * WIDTH, h * LANES:(h + 1) * LANES] = extra

    load_dirs.wait()
    lane = lax.broadcasted_iota(jnp.int32, (PACK, LANES), 1)
    place = lane % WIDTH
    for half in range(2):
        base = k * QUARTER + lax.rem(c + half, 2) * PART
        packed = jnp.zeros((PACK, LANES), F32)
        for g in range(GROUPS):
            rows = pts[pl.ds(pl.multiple_of(base + g * PACK, PACK), PACK), :]
            cbuf[0, half, g * PACK:(g + 1) * PACK, :] = rows
            wide = rows.astype(F32)
            norm = -0.5 * jnp.sum(wide * wide, axis=1, keepdims=True)
            packed = jnp.where(lane // WIDTH == g, norm, packed)
        cbuf[0, half, PART:NORMS, :] = dirs[:, pl.ds(pl.multiple_of(base, LANES), LANES)]
        first, second, third = pieces(packed)
        extra = choose(
            place, [(3, first), (4, second), (5, third)], jnp.where(place < 3, 1.0, 0.0)
        )
        cbuf[0, half, NORMS:MSG, :] = extra.astype(BF)

    pl.semaphore_wait(barrier, 15)

    def copy(n, src, dst, device):
        return pltpu.make_async_remote_copy(
            src_ref=src,
            dst_ref=dst,
            send_sem=send.at[n],
            recv_sem=recv.at[n],
            device_id=device,
            device_id_type=MESH,
        )

    along = {by: copy(by, cbuf.at[0, 0], cbuf.at[by, 0], along_z(-by)) for by in (1, 2, 6, 7)}
    along[3] = copy(3, cbuf.at[2, 0], cbuf.at[3, 0], along_z(-1))
    along[5] = copy(5, cbuf.at[6, 0], cbuf.at[5, 0], along_z(1))
    along[4] = copy(4, cbuf.at[6 - 4 * c, 0], cbuf.at[4, 0], along_z(2 - 4 * c))
    shared = {by: copy(7 + by, cbuf.at[by, 0], cbuf.at[by, 1], mate) for by in range(1, NZ)}
    r_used = pl.ds(0, FEATS + WIDTH)
    rows_x = [
        copy(15 + by, rbuf.at[0, r_used], rbuf.at[by, r_used], along_x(by)) for by in range(1, NX)
    ]
    rows_y = [
        copy(19 + by, rbuf.at[by, r_used], rbuf.at[NX + by, r_used], across(0)) for by in range(NX)
    ]
    back_x = {
        by: copy(23 + by, stage.at[by], obuf.at[by], along_x(NX - by) if by < NX else across(2 * NX - by))
        for by in range(1, 2 * NX)
    }
    back_k = [
        copy(30 + by, fin.at[(k + by) % NK], ybuf.at[by - 1], along_k(by)) for by in range(1, NK)
    ]

    for by in (2, 6, 1, 7):
        along[by].start()
    for by in (1, 3):
        rows_x[by - 1].start()
    rows_y[0].start()
    rows_x[1].start()

    masks = [jnp.where(lane // WIDTH == g, 1.0, 0.0).astype(BF) for g in range(GROUPS)]

    def spread_norms(by, half):
        tile = cbuf[by, half, NORMS:MSG, :]
        for g in range(GROUPS):
            first = half * PART + g * PACK
            maug[by, first:first + PACK, :] = tile * masks[g]

    def pass_on(offsets, onward):
        for by in offsets:
            along[by].wait_recv()
        for by in onward:
            along[by].start()
        for by in offsets:
            shared[by].start()
        for by in offsets:
            spread_norms(by, 0)

    def from_mate(*offsets):
        for by in offsets:
            shared[by].wait_recv()
            spread_norms(by, 1)

    def spread_rows(by):
        tile = rbuf[by, FEATS:FEATS + WIDTH, :]
        for g in range(1, GROUPS):
            rbuf[by, FEATS + g * WIDTH:FEATS + (g + 1) * WIDTH, :] = tile

    def product(sources, by):
        halves = [(n, half) for n in sources for half in range(2)]
        lhs = jnp.concatenate(
            [
                jnp.concatenate([cbuf[n, half, 0:PART, :] for n, half in halves], axis=0),
                jnp.concatenate([maug[n] for n in sources], axis=0),
            ],
            axis=1,
        )
        weights = jnp.concatenate([cbuf[n, half, PART:NORMS, :] for n, half in halves], axis=1)
        power = jnp.dot(lhs, rbuf[by], preferred_element_type=F32)
        value = jnp.minimum(jnp.exp2(power * scale).astype(BF), jnp.ones((), BF))
        return jnp.dot(weights, value, preferred_element_type=F32)

    spread_norms(0, 0)
    spread_norms(0, 1)
    pass_on((1, 7), ())
    for by in (1, 3):
        rows_x[by - 1].wait_recv()
        rows_y[by].start()
        spread_rows(by)
    pass_on((2, 6), (3, 5, 4))
    rows_y[0].wait_recv()
    spread_rows(4)
    from_mate(1, 7)
    for by in (1, 3, 4):
        acc[by] = product((0, 1, 7), by)

    rows_x[1].wait_recv()
    rows_y[2].start()
    spread_rows(2)
    from_mate(2, 6)
    for by in (1, 3, 4):
        acc[by] += product((2, 6), by)
    close = (0, 1, 7, 2, 6)
    acc[2] = product(close, 2)

    rows_y[1].wait_recv()
    spread_rows(5)
    acc[5] = product(close, 5)
    pass_on((3, 5, 4), ())
    rows_y[3].wait_recv()
    spread_rows(7)
    acc[7] = product(close, 7)
    from_mate(3, 5, 4)
    rest = (3, 5, 4)

    def give(*group):
        for by in group:
            value = product(close + rest, by) if by == 6 else acc[by] + product(rest, by)
            stage[by] = value.astype(BF)
        for by in group:
            back_x[by].start()

    give(5, 2)
    give(7, 1)
    rows_y[2].wait_recv()
    spread_rows(6)
    give(6)
    give(3)
    give(4)
    total = product(close + rest, 0)
    for by in (5, 2, 6, 1, 7, 3, 4):
        back_x[by].wait_recv()
        total += obuf[by].astype(F32)
    for h in range(NK):
        fin[h] = total[:, h * LANES:(h + 1) * LANES].astype(BF)
        acc[0, :, h * LANES:(h + 1) * LANES] = total[:, h * LANES:(h + 1) * LANES]
    for by in (2, 1, 3):
        back_k[by - 1].start()
    result = acc[0, :, pl.ds(pl.multiple_of(k * LANES, LANES), LANES)]
    for by in (1, 3, 2):
        back_k[by - 1].wait_recv()
        result += ybuf[by - 1].astype(F32)
    out[...] = result

    groups = (along.values(), shared.values(), rows_x, rows_y, back_x.values(), back_k)
    for group in groups:
        for one in group:
            one.wait_send()


def local(points, directions):
    gamma = 0.5 / points.shape[1]
    turned = pl.pallas_call(
        functools.partial(kernel, 2.0 * gamma * LOG2E),
        out_shape=jax.ShapeDtypeStruct((RHS, LANES), F32),
        in_specs=[pl.BlockSpec(memory_space=pl.ANY)] * 2,
        out_specs=pl.BlockSpec(memory_space=pltpu.VMEM),
        scratch_shapes=[
            pltpu.VMEM((ROWS, FEATS), BF),
            pltpu.VMEM((RHS, ROWS), BF),
            pltpu.VMEM((2 * NX, DEPTH, HALF), BF),
            pltpu.VMEM((NZ, 2, MSG, LANES), BF),
            pltpu.VMEM((NZ, QUARTER, LANES), BF),
            pltpu.VMEM((2 * NX, RHS, HALF), F32),
            pltpu.VMEM((2 * NX, RHS, HALF), BF),
            pltpu.VMEM((2 * NX, RHS, HALF), BF),
            pltpu.VMEM((NK, RHS, LANES), BF),
            pltpu.VMEM((NK - 1, RHS, LANES), BF),
            pltpu.SemaphoreType.DMA((2,)),
            pltpu.SemaphoreType.DMA((34,)),
            pltpu.SemaphoreType.DMA((34,)),
        ],
        compiler_params=pltpu.CompilerParams(
            collective_id=0, has_side_effects=True, vmem_limit_bytes=60 * 2**20
        ),
        name="gauss",
    )(points, directions.T)
    return turned.T


def solution(mesh):
    in_specs = (P("blk", None), P("blk", None))
    out_specs = P(("blk", "layer"), None)
    return jax.shard_map(local, mesh=mesh, in_specs=in_specs, out_specs=out_specs, check_vma=False)
```

```python
import functools

import numpy as np

import jax
import jax.numpy as jnp
from jax import lax
from jax.experimental import pallas as pl
from jax.experimental.pallas import tpu as pltpu
from jax.sharding import PartitionSpec as P

MESH = pl.DeviceIdType.MESH
BF = jnp.bfloat16
F32 = jnp.float32

NX, NP, NZ, NK = 4, 2, 8, 4
ROWS, FEATS, RHS = 1024, 128, 64
HALF = ROWS // 2
LANES = 128
QUARTER = ROWS // NK
PART = QUARTER // 2
GROUPS = 8
PACK = PART // GROUPS
WIDTH = LANES // GROUPS
TILES = PART // LANES
NORMS = PART + TILES * RHS
MSG = NORMS + PACK
DEPTH = 2 * FEATS
LOG2E = float(np.log2(np.e))


def pieces(value):
    first = value.astype(BF).astype(F32)
    rest = value - first
    second = rest.astype(BF).astype(F32)
    third = (rest - second).astype(BF).astype(F32)
    return first, second, third


def choose(index, values, others):
    result = others
    for at, value in values:
        result = jnp.where(index == at, value, result)
    return result


def kernel(scale, pts_hbm, dirs_hbm, out, pts, dirs, rbuf, cbuf, maug, acc, stage, obuf, fin, ybuf, load, send, recv):
    blk, layer = lax.axis_index("blk"), lax.axis_index("layer")
    x, p, z = blk % NX, (blk // NX) % NP, blk // (NX * NP)
    k, c = layer // 2, layer % 2

    def at(xx=x, pp=p, zz=z, kk=k, cc=c):
        return ((zz * NP + pp) * NX + xx, kk * 2 + cc)

    def along_x(by):
        return at(xx=(x + by) % NX)

    def along_z(by):
        return at(zz=(z + by + 2 * NZ) % NZ)

    def along_k(by):
        return at(kk=(k + by) % NK)

    mate = at(cc=1 - c)
    pair_k = (k + c * (2 * p - 1) + NK) % NK

    def across(by):
        return at(xx=(x + by) % NX, pp=1 - p, kk=pair_k)

    load_pts = pltpu.make_async_copy(pts_hbm, pts, load.at[0])
    load_dirs = pltpu.make_async_copy(dirs_hbm, dirs, load.at[1])
    load_pts.start()
    load_dirs.start()

    barrier = pltpu.get_barrier_semaphore()

    def greet(device):
        pl.semaphore_signal(barrier, inc=1, device_id=device, device_id_type=MESH)

    for by in (2, -2, 1, -1):
        greet(along_z(by))
    for by in range(1, NK):
        greet(along_k(by))
    for by in range(1, NX):
        greet(along_x(by))
    for by in range(NX):
        greet(across(by))
    greet(mate)

    load_pts.wait()

    row = lax.broadcasted_iota(jnp.int32, (WIDTH, LANES), 0)
    for h in range(NK):
        rows = pts[pl.ds(pl.multiple_of((2 * h + c) * LANES, LANES), LANES), :]
        turned = rows.astype(F32).T
        rbuf[0, 0:FEATS, h * LANES:(h + 1) * LANES] = turned.astype(BF)
        norm = -0.5 * jnp.sum(turned * turned, axis=0, keepdims=True)
        first, second, third = pieces(norm)
        extra = choose(
            row, [(0, first), (1, second), (2, third)], jnp.where(row < 6, 1.0, 0.0)
        ).astype(BF)
        for g in range(GROUPS):
            rbuf[0, FEATS + g * WIDTH:FEATS + (g + 1) * WIDTH, h * LANES:(h + 1) * LANES] = extra

    pl.semaphore_wait(barrier, 15)

    def copy(n, src, dst, device):
        return pltpu.make_async_remote_copy(
            src_ref=src,
            dst_ref=dst,
            send_sem=send.at[n],
            recv_sem=recv.at[n],
            device_id=device,
            device_id_type=MESH,
        )

    along = {by: copy(by, cbuf.at[0, 0], cbuf.at[by, 0], along_z(-by)) for by in (1, 2, 6, 7)}
    along[3] = copy(3, cbuf.at[2, 0], cbuf.at[3, 0], along_z(-1))
    along[5] = copy(5, cbuf.at[6, 0], cbuf.at[5, 0], along_z(1))
    along[4] = copy(4, cbuf.at[6 - 4 * c, 0], cbuf.at[4, 0], along_z(2 - 4 * c))
    shared = {by: copy(7 + by, cbuf.at[by, 0], cbuf.at[by, 1], mate) for by in range(1, NZ)}
    r_used = pl.ds(0, FEATS + WIDTH)
    rows_x = [
        copy(15 + by, rbuf.at[0, r_used], rbuf.at[by, r_used], along_x(by)) for by in range(1, NX)
    ]
    rows_y = [
        copy(19 + by, rbuf.at[by, r_used], rbuf.at[NX + by, r_used], across(0)) for by in range(NX)
    ]
    back_x = {
        by: copy(23 + by, stage.at[by], obuf.at[by], along_x(NX - by) if by < NX else across(2 * NX - by))
        for by in range(1, 2 * NX)
    }
    back_k = [
        copy(30 + by, fin.at[(k + by) % NK], ybuf.at[by - 1], along_k(by)) for by in range(1, NK)
    ]

    for by in (1, 3):
        rows_x[by - 1].start()
    rows_y[0].start()

    load_dirs.wait()
    lane = lax.broadcasted_iota(jnp.int32, (PACK, LANES), 1)
    place = lane % WIDTH
    for half in range(2):
        base = k * QUARTER + lax.rem(c + half, 2) * PART
        packed = jnp.zeros((PACK, LANES), F32)
        for g in range(GROUPS):
            rows = pts[pl.ds(pl.multiple_of(base + g * PACK, PACK), PACK), :]
            cbuf[0, half, g * PACK:(g + 1) * PACK, :] = rows
            wide = rows.astype(F32)
            norm = -0.5 * jnp.sum(wide * wide, axis=1, keepdims=True)
            packed = jnp.where(lane // WIDTH == g, norm, packed)
        cbuf[0, half, PART:NORMS, :] = dirs[:, pl.ds(pl.multiple_of(base, LANES), LANES)]
        first, second, third = pieces(packed)
        extra = choose(
            place, [(3, first), (4, second), (5, third)], jnp.where(place < 3, 1.0, 0.0)
        )
        cbuf[0, half, NORMS:MSG, :] = extra.astype(BF)

    for by in (1, 7, 2, 6):
        along[by].start()
    rows_x[1].start()

    masks = [jnp.where(lane // WIDTH == g, 1.0, 0.0).astype(BF) for g in range(GROUPS)]

    def spread_norms(by, half):
        tile = cbuf[by, half, NORMS:MSG, :]
        for g in range(GROUPS):
            first = half * PART + g * PACK
            maug[by, first:first + PACK, :] = tile * masks[g]

    def pass_on(offsets, onward):
        for by in offsets:
            along[by].wait_recv()
        for by in onward:
            along[by].start()
        for by in offsets:
            shared[by].start()
        for by in offsets:
            spread_norms(by, 0)

    def from_mate(*offsets):
        for by in offsets:
            shared[by].wait_recv()
            spread_norms(by, 1)

    def spread_rows(by):
        tile = rbuf[by, FEATS:FEATS + WIDTH, :]
        for g in range(1, GROUPS):
            rbuf[by, FEATS + g * WIDTH:FEATS + (g + 1) * WIDTH, :] = tile

    def product(sources, by):
        halves = [(n, half) for n in sources for half in range(2)]
        lhs = jnp.concatenate(
            [
                jnp.concatenate([cbuf[n, half, 0:PART, :] for n, half in halves], axis=0),
                jnp.concatenate([maug[n] for n in sources], axis=0),
            ],
            axis=1,
        )
        weights = jnp.concatenate([cbuf[n, half, PART:NORMS, :] for n, half in halves], axis=1)
        power = jnp.dot(lhs, rbuf[by], preferred_element_type=F32)
        value = jnp.minimum(jnp.exp2(power * scale).astype(BF), jnp.ones((), BF))
        return jnp.dot(weights, value, preferred_element_type=F32)

    spread_norms(0, 0)
    spread_norms(0, 1)
    pass_on((1, 7), ())
    for by in (1, 3):
        rows_x[by - 1].wait_recv()
        rows_y[by].start()
        spread_rows(by)
    pass_on((2, 6), (3, 5, 4))
    rows_y[0].wait_recv()
    spread_rows(4)
    from_mate(1, 7)
    for by in (1, 3, 4):
        acc[by] = product((0, 1, 7), by)

    rows_x[1].wait_recv()
    rows_y[2].start()
    spread_rows(2)
    from_mate(2, 6)
    for by in (1, 3, 4):
        acc[by] += product((2, 6), by)
    close = (0, 1, 7, 2, 6)
    acc[2] = product(close, 2)

    rows_y[1].wait_recv()
    spread_rows(5)
    acc[5] = product(close, 5)
    pass_on((3, 5, 4), ())
    rows_y[3].wait_recv()
    spread_rows(7)
    acc[7] = product(close, 7)
    from_mate(3, 5, 4)
    rest = (3, 5, 4)

    def give(*group):
        for by in group:
            value = product(close + rest, by) if by == 6 else acc[by] + product(rest, by)
            stage[by] = value.astype(BF)
        for by in group:
            back_x[by].start()

    give(5, 2)
    give(7, 1)
    rows_y[2].wait_recv()
    spread_rows(6)
    give(6)
    give(3)
    give(4)
    total = product(close + rest, 0)
    for by in (5, 2, 6, 1, 7, 3, 4):
        back_x[by].wait_recv()
        total += obuf[by].astype(F32)
    for h in range(NK):
        fin[h] = total[:, h * LANES:(h + 1) * LANES].astype(BF)
        acc[0, :, h * LANES:(h + 1) * LANES] = total[:, h * LANES:(h + 1) * LANES]
    for by in (2, 1, 3):
        back_k[by - 1].start()
    result = acc[0, :, pl.ds(pl.multiple_of(k * LANES, LANES), LANES)]
    for by in (1, 3, 2):
        back_k[by - 1].wait_recv()
        result += ybuf[by - 1].astype(F32)
    out[...] = result

    groups = (along.values(), shared.values(), rows_x, rows_y, back_x.values(), back_k)
    for group in groups:
        for one in group:
            one.wait_send()


def local(points, directions):
    gamma = 0.5 / points.shape[1]
    turned = pl.pallas_call(
        functools.partial(kernel, 2.0 * gamma * LOG2E),
        out_shape=jax.ShapeDtypeStruct((RHS, LANES), F32),
        in_specs=[pl.BlockSpec(memory_space=pl.ANY)] * 2,
        out_specs=pl.BlockSpec(memory_space=pltpu.VMEM),
        scratch_shapes=[
            pltpu.VMEM((ROWS, FEATS), BF),
            pltpu.VMEM((RHS, ROWS), BF),
            pltpu.VMEM((2 * NX, DEPTH, HALF), BF),
            pltpu.VMEM((NZ, 2, MSG, LANES), BF),
            pltpu.VMEM((NZ, QUARTER, LANES), BF),
            pltpu.VMEM((2 * NX, RHS, HALF), F32),
            pltpu.VMEM((2 * NX, RHS, HALF), BF),
            pltpu.VMEM((2 * NX, RHS, HALF), BF),
            pltpu.VMEM((NK, RHS, LANES), BF),
            pltpu.VMEM((NK - 1, RHS, LANES), BF),
            pltpu.SemaphoreType.DMA((2,)),
            pltpu.SemaphoreType.DMA((34,)),
            pltpu.SemaphoreType.DMA((34,)),
        ],
        compiler_params=pltpu.CompilerParams(
            collective_id=0, has_side_effects=True, vmem_limit_bytes=60 * 2**20
        ),
        name="gauss",
    )(points, directions.T)
    return turned.T


def solution(mesh):
    in_specs = (P("blk", None), P("blk", None))
    out_specs = P(("blk", "layer"), None)
    return jax.shard_map(local, mesh=mesh, in_specs=in_specs, out_specs=out_specs, check_vma=False)
```

```python
import functools

import numpy as np

import jax
import jax.numpy as jnp
from jax import lax
from jax.experimental import pallas as pl
from jax.experimental.pallas import tpu as pltpu
from jax.sharding import PartitionSpec as P

MESH = pl.DeviceIdType.MESH
BF = jnp.bfloat16
F32 = jnp.float32

NX, NP, NZ, NK = 4, 2, 8, 4
ROWS, FEATS, RHS = 1024, 128, 64
HALF = ROWS // 2
LANES = 128
QUARTER = ROWS // NK
PART = QUARTER // 2
GROUPS = 8
PACK = PART // GROUPS
WIDTH = LANES // GROUPS
TILES = PART // LANES
NORMS = PART + TILES * RHS
MSG = NORMS + PACK
DEPTH = 2 * FEATS
LOG2E = float(np.log2(np.e))


def pieces(value):
    first = value.astype(BF).astype(F32)
    rest = value - first
    second = rest.astype(BF).astype(F32)
    third = (rest - second).astype(BF).astype(F32)
    return first, second, third


def choose(index, values, others):
    result = others
    for at, value in values:
        result = jnp.where(index == at, value, result)
    return result


def kernel(scale, pts_hbm, dirs_hbm, out, pts, dirs, rbuf, cbuf, maug, acc, stage, obuf, fin, ybuf, load, send, recv):
    blk, layer = lax.axis_index("blk"), lax.axis_index("layer")
    x, p, z = blk % NX, (blk // NX) % NP, blk // (NX * NP)
    k, c = layer // 2, layer % 2

    def at(xx=x, pp=p, zz=z, kk=k, cc=c):
        return ((zz * NP + pp) * NX + xx, kk * 2 + cc)

    def along_x(by):
        return at(xx=(x + by) % NX)

    def along_z(by):
        return at(zz=(z + by + 2 * NZ) % NZ)

    def along_k(by):
        return at(kk=(k + by) % NK)

    mate = at(cc=1 - c)
    pair_k = (k + c * (2 * p - 1) + NK) % NK

    def across(by):
        return at(xx=(x + by) % NX, pp=1 - p, kk=pair_k)

    load_pts = pltpu.make_async_copy(pts_hbm, pts, load.at[0])
    load_dirs = pltpu.make_async_copy(dirs_hbm, dirs, load.at[1])
    load_pts.start()
    load_dirs.start()

    barrier = pltpu.get_barrier_semaphore()

    def greet(device):
        pl.semaphore_signal(barrier, inc=1, device_id=device, device_id_type=MESH)

    for by in (2, 1, 3):
        greet(along_k(by))
        greet(across(by))
    for by in (2, -2, 1, -1):
        greet(along_z(by))
    for by in (2, 1, 3):
        greet(along_x(by))
    greet(across(0))
    greet(mate)

    load_pts.wait()

    row = lax.broadcasted_iota(jnp.int32, (WIDTH, LANES), 0)
    for h in range(NK):
        rows = pts[pl.ds(pl.multiple_of((2 * h + c) * LANES, LANES), LANES), :]
        turned = rows.astype(F32).T
        rbuf[0, 0:FEATS, h * LANES:(h + 1) * LANES] = turned.astype(BF)
        norm = -0.5 * jnp.sum(turned * turned, axis=0, keepdims=True)
        first, second, third = pieces(norm)
        extra = choose(
            row, [(0, first), (1, second), (2, third)], jnp.where(row < 6, 1.0, 0.0)
        ).astype(BF)
        for g in range(GROUPS):
            rbuf[0, FEATS + g * WIDTH:FEATS + (g + 1) * WIDTH, h * LANES:(h + 1) * LANES] = extra

    pl.semaphore_wait(barrier, 15)

    def copy(n, src, dst, device):
        return pltpu.make_async_remote_copy(
            src_ref=src,
            dst_ref=dst,
            send_sem=send.at[n],
            recv_sem=recv.at[n],
            device_id=device,
            device_id_type=MESH,
        )

    along = {by: copy(by, cbuf.at[0, 0], cbuf.at[by, 0], along_z(-by)) for by in (1, 2, 6, 7)}
    along[3] = copy(3, cbuf.at[2, 0], cbuf.at[3, 0], along_z(-1))
    along[5] = copy(5, cbuf.at[6, 0], cbuf.at[5, 0], along_z(1))
    along[4] = copy(4, cbuf.at[6 - 4 * c, 0], cbuf.at[4, 0], along_z(2 - 4 * c))
    shared = {by: copy(7 + by, cbuf.at[by, 0], cbuf.at[by, 1], mate) for by in range(1, NZ)}
    r_used = pl.ds(0, FEATS + WIDTH)
    rows_x = [
        copy(15 + by, rbuf.at[0, r_used], rbuf.at[by, r_used], along_x(by)) for by in range(1, NX)
    ]
    rows_y = [
        copy(19 + by, rbuf.at[by, r_used], rbuf.at[NX + by, r_used], across(0)) for by in range(NX)
    ]
    back_x = {
        by: copy(23 + by, stage.at[by], obuf.at[by], along_x(NX - by) if by < NX else across(2 * NX - by))
        for by in range(1, 2 * NX)
    }
    back_k = [
        copy(30 + by, fin.at[(k + by) % NK], ybuf.at[by - 1], along_k(by)) for by in range(1, NK)
    ]

    for by in (1, 3):
        rows_x[by - 1].start()
    rows_y[0].start()

    load_dirs.wait()
    lane = lax.broadcasted_iota(jnp.int32, (PACK, LANES), 1)
    place = lane % WIDTH
    for half in range(2):
        base = k * QUARTER + lax.rem(c + half, 2) * PART
        packed = jnp.zeros((PACK, LANES), F32)
        for g in range(GROUPS):
            rows = pts[pl.ds(pl.multiple_of(base + g * PACK, PACK), PACK), :]
            cbuf[0, half, g * PACK:(g + 1) * PACK, :] = rows
            wide = rows.astype(F32)
            norm = -0.5 * jnp.sum(wide * wide, axis=1, keepdims=True)
            packed = jnp.where(lane // WIDTH == g, norm, packed)
        cbuf[0, half, PART:NORMS, :] = dirs[:, pl.ds(pl.multiple_of(base, LANES), LANES)]
        first, second, third = pieces(packed)
        extra = choose(
            place, [(3, first), (4, second), (5, third)], jnp.where(place < 3, 1.0, 0.0)
        )
        cbuf[0, half, NORMS:MSG, :] = extra.astype(BF)

    for by in (1, 7, 2, 6):
        along[by].start()
    rows_x[1].start()

    masks = [jnp.where(lane // WIDTH == g, 1.0, 0.0).astype(BF) for g in range(GROUPS)]

    def spread_norms(by, half):
        tile = cbuf[by, half, NORMS:MSG, :]
        for g in range(GROUPS):
            first = half * PART + g * PACK
            maug[by, first:first + PACK, :] = tile * masks[g]

    def pass_on(offsets, onward):
        for by in offsets:
            along[by].wait_recv()
        for by in onward:
            along[by].start()
        for by in offsets:
            shared[by].start()
        for by in offsets:
            spread_norms(by, 0)

    def from_mate(*offsets):
        for by in offsets:
            shared[by].wait_recv()
            spread_norms(by, 1)

    def spread_rows(by):
        tile = rbuf[by, FEATS:FEATS + WIDTH, :]
        for g in range(1, GROUPS):
            rbuf[by, FEATS + g * WIDTH:FEATS + (g + 1) * WIDTH, :] = tile

    def product(sources, by):
        halves = [(n, half) for n in sources for half in range(2)]
        lhs = jnp.concatenate(
            [
                jnp.concatenate([cbuf[n, half, 0:PART, :] for n, half in halves], axis=0),
                jnp.concatenate([maug[n] for n in sources], axis=0),
            ],
            axis=1,
        )
        weights = jnp.concatenate([cbuf[n, half, PART:NORMS, :] for n, half in halves], axis=1)
        power = jnp.dot(lhs, rbuf[by], preferred_element_type=F32)
        value = jnp.minimum(jnp.exp2(power * scale).astype(BF), jnp.ones((), BF))
        return jnp.dot(weights, value, preferred_element_type=F32)

    spread_norms(0, 0)
    spread_norms(0, 1)
    pass_on((1, 7), ())
    for by in (1, 3):
        rows_x[by - 1].wait_recv()
        rows_y[by].start()
        spread_rows(by)
    pass_on((2, 6), (3, 5, 4))
    rows_y[0].wait_recv()
    spread_rows(4)
    from_mate(1, 7)
    for by in (1, 3, 4):
        acc[by] = product((0, 1, 7), by)

    rows_x[1].wait_recv()
    rows_y[2].start()
    spread_rows(2)
    from_mate(2, 6)
    for by in (1, 3, 4):
        acc[by] += product((2, 6), by)
    close = (0, 1, 7, 2, 6)
    acc[2] = product(close, 2)

    rows_y[1].wait_recv()
    spread_rows(5)
    acc[5] = product(close, 5)
    pass_on((3, 5, 4), ())
    rows_y[3].wait_recv()
    spread_rows(7)
    acc[7] = product(close, 7)
    from_mate(3, 5, 4)
    rest = (3, 5, 4)

    def give(*group):
        for by in group:
            value = product(close + rest, by) if by == 6 else acc[by] + product(rest, by)
            stage[by] = value.astype(BF)
        for by in group:
            back_x[by].start()

    give(5, 2)
    give(7, 1)
    rows_y[2].wait_recv()
    spread_rows(6)
    give(6)
    give(3)
    give(4)
    total = product(close + rest, 0)
    for by in (5, 2, 6, 1, 7, 3, 4):
        back_x[by].wait_recv()
        total += obuf[by].astype(F32)
    for h in range(NK):
        fin[h] = total[:, h * LANES:(h + 1) * LANES].astype(BF)
        acc[0, :, h * LANES:(h + 1) * LANES] = total[:, h * LANES:(h + 1) * LANES]
    for by in (2, 1, 3):
        back_k[by - 1].start()
    result = acc[0, :, pl.ds(pl.multiple_of(k * LANES, LANES), LANES)]
    for by in (1, 3, 2):
        back_k[by - 1].wait_recv()
        result += ybuf[by - 1].astype(F32)
    out[...] = result

    groups = (along.values(), shared.values(), rows_x, rows_y, back_x.values(), back_k)
    for group in groups:
        for one in group:
            one.wait_send()


def local(points, directions):
    gamma = 0.5 / points.shape[1]
    turned = pl.pallas_call(
        functools.partial(kernel, 2.0 * gamma * LOG2E),
        out_shape=jax.ShapeDtypeStruct((RHS, LANES), F32),
        in_specs=[pl.BlockSpec(memory_space=pl.ANY)] * 2,
        out_specs=pl.BlockSpec(memory_space=pltpu.VMEM),
        scratch_shapes=[
            pltpu.VMEM((ROWS, FEATS), BF),
            pltpu.VMEM((RHS, ROWS), BF),
            pltpu.VMEM((2 * NX, DEPTH, HALF), BF),
            pltpu.VMEM((NZ, 2, MSG, LANES), BF),
            pltpu.VMEM((NZ, QUARTER, LANES), BF),
            pltpu.VMEM((2 * NX, RHS, HALF), F32),
            pltpu.VMEM((2 * NX, RHS, HALF), BF),
            pltpu.VMEM((2 * NX, RHS, HALF), BF),
            pltpu.VMEM((NK, RHS, LANES), BF),
            pltpu.VMEM((NK - 1, RHS, LANES), BF),
            pltpu.SemaphoreType.DMA((2,)),
            pltpu.SemaphoreType.DMA((34,)),
            pltpu.SemaphoreType.DMA((34,)),
        ],
        compiler_params=pltpu.CompilerParams(
            collective_id=0, has_side_effects=True, vmem_limit_bytes=60 * 2**20
        ),
        name="gauss",
    )(points, directions.T)
    return turned.T


def solution(mesh):
    in_specs = (P("blk", None), P("blk", None))
    out_specs = P(("blk", "layer"), None)
    return jax.shard_map(local, mesh=mesh, in_specs=in_specs, out_specs=out_specs, check_vma=False)
```
